512 devices in a mesh: dp: 16 (over z), fsdp: 8 (over y, x_hi), tensor: 4 (over x_lo, core).
Axes of the slice: x: 4 (x_hi: 2, x_lo: 2; x = x_hi * 2 + x_lo), y: 4, z: 16, core: 2. Of those that a mesh axis runs over, the one named last changes fastest.
Arguments:
- tokens: bfloat16 [32768, 2560], P(('dp', 'fsdp')), may hold values from -6 to 6
- cotangent: bfloat16 [32768, 7168], P(('dp', 'fsdp'), 'tensor'), may hold values from -6 to 6
- weight: bfloat16 [2560, 7168], P(('dp', 'fsdp'), 'tensor'), may hold values from -0.125 to 0.125
- basis: bfloat16 [2560, 256], P(('dp', 'fsdp')), may hold values from -0.125 to 0.125
- first_moment: float32 [256, 7168], P(('dp', 'fsdp'), 'tensor'), may hold values from -0.0016572815 to 0.0016572815
- second_moment: float32 [256, 7168], P(('dp', 'fsdp'), 'tensor'), may hold values from 3.0517578e-07 to 6.1035156e-06
Outputs:
- token_grad: bfloat16 [32768, 2560], P(('dp', 'fsdp'))
- new_weight: bfloat16 [2560, 7168], P(('dp', 'fsdp'), 'tensor')
- new_first_moment: float32 [256, 7168], P(('dp', 'fsdp'), 'tensor')
- new_second_moment: float32 [256, 7168], P(('dp', 'fsdp'), 'tensor')
The draws below stay inside these ranges and needn't reach their ends.
All inputs are finite; a program needn't handle non-finite values.
Results may differ from the reference program's by a relative error of at most 0.015.
Values may be sent and summed in bfloat16 or wider, within the bound.
No kernel may reach another device: no remote copies, remote signals or barrier semaphores. Data moves between devices by JAX's collectives and lax.ppermute only.
A program may use at most 64 MiB of HBM per device.

```python
import math
import jax
import jax.numpy as jnp
from jax import lax

D = 2560
FW = 7168
R = 256
ADAM_STEP = 10
TOK_DEV = 256
TOKENS = 32768
N_DP = 16
N_FSDP = 8
N_TENSOR = 4


def draw_first_moment(key, part):
    key = jax.random.fold_in(key, 11)
    values = jax.random.truncated_normal(key, -6.0, 6.0, (R, FW), jnp.float32)
    return 0.05 * values / jnp.sqrt(jnp.float32(TOKENS))


def draw_second_moment(key, part):
    key = jax.random.fold_in(key, 12)
    spread = jax.random.uniform(key, (R, FW), jnp.float32, math.log(0.01), math.log(0.2))
    return jnp.exp(spread) / jnp.float32(TOKENS)


def block_levels(stream_key, extent, pieces, low, high):
    def one(position, parts):
        steps = jax.random.uniform(jax.random.fold_in(jax.random.fold_in(stream_key, 6), position), (parts,), jnp.float32, low / len(pieces), high / len(pieces))
        return jnp.repeat(jnp.exp(steps), extent[position] // parts).reshape((-1,) + (1,) * (len(extent) - position - 1))

    gain = one(*pieces[0])
    for cut in pieces[1:]:
        gain = gain * one(*cut)
    return gain


def normal_values(key, shape, scale, bound, cuts=(), kind=jnp.bfloat16):
    entries = scale * jax.random.normal(key, shape, jnp.float32)
    if cuts:
        entries = entries * block_levels(key, shape, cuts, -0.22, 0.18)
    return jnp.clip(entries, -bound, bound).astype(kind)


def setup_inputs(seed: int = 0) -> dict:
    key_list = jax.random.split(jax.random.key(seed), 7)
    tokens = normal_values(key_list[0], (TOKENS, D), 1.0, 6.0, ((0, 128),))
    cotangent = normal_values(key_list[1], (TOKENS, FW), 1.0, 6.0, ((0, 128), (1, 4)))
    weight = normal_values(key_list[2], (D, FW), D ** -0.5, 0.125, ((0, 128), (1, 4)))
    basis = normal_values(key_list[3], (D, R), D ** -0.5, 0.125, ((0, 128),))
    first_moment = draw_first_moment(jax.random.fold_in(key_list[6], 71), 0)
    second_moment = draw_second_moment(jax.random.fold_in(key_list[6], 71), 0)
    return dict(tokens=tokens, cotangent=cotangent, weight=weight, basis=basis, first_moment=first_moment, second_moment=second_moment)


BETA_ONE = 0.9
BETA_TWO = 0.95
EPSILON = 1e-08
LEARN_RATE = 0.01

def silu_slope(preact):
    logistic = jax.nn.sigmoid(preact)
    return logistic * (1.0 + preact * (1.0 - logistic))

def reference(tokens, cotangent, weight, basis, first_moment, second_moment):
    groups = N_DP * N_FSDP
    quarter = FW // N_TENSOR
    token_blocks = tokens.reshape(groups, TOK_DEV, D)
    cotangent_blocks = cotangent.reshape(groups, TOK_DEV, FW)

    def advance(running, sliced):
        block_tokens, block_cotangent = sliced
        preact = jnp.dot(block_tokens, weight, preferred_element_type=jnp.float32)
        grad_pre = (block_cotangent.astype(jnp.float32) * silu_slope(preact)).astype(jnp.bfloat16)
        summed = jnp.zeros((TOK_DEV, D), jnp.float32)
        for index in range(N_TENSOR):
            quarter_sum = lax.dot_general(grad_pre[:, index * quarter:(index + 1) * quarter], weight[:, index * quarter:(index + 1) * quarter], (((1,), (1,)), ((), ())), preferred_element_type=jnp.float32)
            summed = summed + lax.optimization_barrier(quarter_sum.astype(jnp.bfloat16)).astype(jnp.float32)
        projected = jnp.dot(block_tokens, basis, preferred_element_type=jnp.float32).astype(jnp.bfloat16)
        running = running + lax.dot_general(projected, grad_pre, (((0,), (0,)), ((), ())), preferred_element_type=jnp.float32)
        return (running, summed.astype(jnp.bfloat16))
    grad_sum, token_grad = lax.scan(advance, jnp.zeros((R, FW), jnp.float32), (token_blocks, cotangent_blocks))
    token_grad = token_grad.reshape(TOKENS, D)
    grad_low = grad_sum / TOKENS
    new_first_moment = BETA_ONE * first_moment + (1.0 - BETA_ONE) * grad_low
    new_second_moment = BETA_TWO * second_moment + (1.0 - BETA_TWO) * grad_low * grad_low
    first_hat = new_first_moment / (1.0 - BETA_ONE ** ADAM_STEP)
    second_hat = new_second_moment / (1.0 - BETA_TWO ** ADAM_STEP)
    direction = (first_hat / (jnp.sqrt(second_hat) + EPSILON)).astype(jnp.bfloat16)
    update = jnp.dot(basis, direction, preferred_element_type=jnp.float32)
    new_weight = (weight.astype(jnp.float32) - LEARN_RATE * update).astype(jnp.bfloat16)
    return (token_grad, new_weight, new_first_moment, new_second_moment)
```

```python
import jax
import jax.numpy as jnp
from jax import lax
from jax.sharding import PartitionSpec as P

ADAM_STEP = 10


BETA_ONE = 0.9
BETA_TWO = 0.95
EPSILON = 1e-08
LEARN_RATE = 0.01


def silu_slope(preact):
    logistic = jax.nn.sigmoid(preact)
    return logistic * (1.0 + preact * (1.0 - logistic))


def spread(block, axis):
    count = lax.axis_size(axis)
    copies = jnp.broadcast_to(block[None], (count,) + block.shape)
    return lax.all_to_all(copies, axis, 0, 0, tiled=True)


def local(tokens, cotangent, weight, basis, first_moment, second_moment):
    f32, bf16 = jnp.float32, jnp.bfloat16
    outer, inner, quarters = lax.axis_size("dp"), lax.axis_size("fsdp"), lax.axis_size("tensor")
    rows, width = weight.shape
    rank = basis.shape[1]
    share = rank // (outer * inner)
    basis_perm = basis.reshape(rows, outer, inner, share).transpose(0, 2, 1, 3).reshape(rows, rank)
    part = rank // quarters
    basis_part = lax.dynamic_slice_in_dim(basis_perm, lax.axis_index("tensor") * part, part, 1)

    weight_plane = spread(weight, "fsdp").reshape(inner * rows, width)
    full_weight = lax.all_gather(weight_plane, "dp", axis=0, tiled=True)
    basis_plane = spread(basis_part, "fsdp").reshape(inner * rows, part)
    full_basis = spread(basis_plane, "dp").reshape(outer * inner * rows, part)
    projected_part = lax.dot_general(
        full_basis, tokens, (((0,), (1,)), ((), ())), preferred_element_type=f32
    ).astype(bf16)
    projected = spread(projected_part, "tensor").reshape(rank, tokens.shape[0])

    preact = jnp.dot(tokens, full_weight, preferred_element_type=f32)
    grad_pre = (cotangent.astype(f32) * silu_slope(preact)).astype(bf16)
    grad_part = jnp.dot(projected, grad_pre, preferred_element_type=f32).astype(bf16)
    partial_rows = lax.dot_general(
        grad_pre, full_weight, (((1,), (1,)), ((), ())), preferred_element_type=f32
    )
    token_grad = lax.psum(partial_rows.astype(bf16), "tensor")

    landed = lax.all_to_all(grad_part.reshape(inner, outer * share, width), "fsdp", 0, 0, tiled=True)
    inner_sum = jnp.sum(landed.astype(f32), axis=0)
    landed = lax.all_to_all(inner_sum.reshape(outer, share, width), "dp", 0, 0, tiled=True)
    reduced = jnp.sum(landed, axis=0)

    token_count = tokens.shape[0] * outer * inner
    grad_low = reduced / float(token_count)
    new_first_moment = BETA_ONE * first_moment + (1.0 - BETA_ONE) * grad_low
    new_second_moment = BETA_TWO * second_moment + (1.0 - BETA_TWO) * grad_low * grad_low
    first_hat = new_first_moment / (1.0 - BETA_ONE**ADAM_STEP)
    second_hat = new_second_moment / (1.0 - BETA_TWO**ADAM_STEP)
    direction = (first_hat / (jnp.sqrt(second_hat) + EPSILON)).astype(bf16)
    column = spread(direction, "dp").reshape(outer * share, width)
    full_direction = spread(column, "fsdp").reshape(rank, width)
    update = jnp.dot(basis_perm, full_direction, preferred_element_type=f32)
    new_weight = (weight.astype(f32) - LEARN_RATE * update).astype(bf16)
    return (token_grad, new_weight, new_first_moment, new_second_moment)


def solution(mesh):
    in_specs = (
        P(("dp", "fsdp"), None),
        P(("dp", "fsdp"), "tensor"),
        P(("dp", "fsdp"), "tensor"),
        P(("dp", "fsdp"), None),
        P(("dp", "fsdp"), "tensor"),
        P(("dp", "fsdp"), "tensor"),
    )
    out_specs = (
        P(("dp", "fsdp"), None),
        P(("dp", "fsdp"), "tensor"),
        P(("dp", "fsdp"), "tensor"),
        P(("dp", "fsdp"), "tensor"),
    )
    return jax.shard_map(local, mesh=mesh, in_specs=in_specs, out_specs=out_specs, check_vma=False)
```

```python
import jax
import jax.numpy as jnp
from jax import lax
from jax.sharding import PartitionSpec as P

ADAM_STEP = 10


BETA_ONE = 0.9
BETA_TWO = 0.95
EPSILON = 1e-08
LEARN_RATE = 0.01
RING = 4
PAIR = 2


def silu_slope(preact):
    logistic = jax.nn.sigmoid(preact)
    return logistic * (1.0 + preact * (1.0 - logistic))


def spread(block, axis, groups=None):
    count = lax.axis_size(axis) if groups is None else len(groups[0])
    copies = jnp.broadcast_to(block[None], (count,) + block.shape)
    return lax.all_to_all(copies, axis, 0, 0, tiled=True, axis_index_groups=groups)


def ring_of_four(block, axis, step, place):
    count = lax.axis_size(axis)
    ahead = [((i + step) % count, i) for i in range(count)]
    behind = [(i, (i + step) % count) for i in range(count)]
    half = block.shape[0] // 2
    following = lax.ppermute(block, axis, ahead)
    preceding = lax.ppermute(block, axis, behind)
    far_front = lax.ppermute(following[:half], axis, ahead)
    far_back = lax.ppermute(preceding[half:], axis, behind)
    far = jnp.concatenate([far_front, far_back], axis=0)
    stacked = jnp.stack([block, following, far, preceding])
    return lambda wanted: lax.dynamic_index_in_dim(
        stacked, lax.rem(wanted - place + RING, RING), 0, keepdims=False
    )


def local(tokens, cotangent, weight, basis, first_moment, second_moment):
    f32, bf16 = jnp.float32, jnp.bfloat16
    outer, inner, quarters = lax.axis_size("dp"), lax.axis_size("fsdp"), lax.axis_size("tensor")
    rows, width = weight.shape
    rank = basis.shape[1]
    depth = outer * inner * rows
    share = rank // (outer * inner)
    basis_perm = basis.reshape(rows, outer, inner, share).transpose(0, 2, 1, 3).reshape(rows, rank)
    part = rank // quarters
    basis_part = lax.dynamic_slice_in_dim(basis_perm, lax.axis_index("tensor") * part, part, 1)

    pairs = [[PAIR * y + x for x in range(PAIR)] for y in range(RING)]
    columns = [[PAIR * y + x for y in range(RING)] for x in range(PAIR)]
    strides = [[i + RING * j for j in range(outer // RING)] for i in range(RING)]
    pair_rows = PAIR * rows
    both = jnp.concatenate([weight, basis_part], axis=1)
    block = spread(both, "fsdp", pairs).reshape(pair_rows, width + part)
    half = width // 2
    plane = spread(block[:, :half], "fsdp", columns).reshape(inner * rows, half)
    weight_a = lax.all_gather(plane, "dp", axis=0, tiled=True)
    second = block[:, half:]
    strided = spread(second, "dp", strides)
    place = lax.rem(lax.axis_index("dp"), RING)
    pick = ring_of_four(strided, "dp", 1, place)
    line = jnp.stack([pick(r) for r in range(RING)], axis=1).reshape(outer, pair_rows, half + part)
    pick = ring_of_four(line, "fsdp", PAIR, lax.axis_index("fsdp") // PAIR)
    full_b = jnp.stack([pick(r) for r in range(RING)], axis=1).reshape(depth, half + part)
    weight_b, full_basis = full_b[:, :half], full_b[:, half:]

    projected_part = lax.dot_general(
        full_basis, tokens, (((0,), (1,)), ((), ())), preferred_element_type=f32
    ).astype(bf16)
    projected = spread(projected_part, "tensor").reshape(rank, tokens.shape[0])

    grad_pre, grad_part = [], []
    for index, side in enumerate((weight_a, weight_b)):
        preact = jnp.dot(tokens, side, preferred_element_type=f32)
        wanted = cotangent[:, index * half : (index + 1) * half].astype(f32)
        grad_pre.append((wanted * silu_slope(preact)).astype(bf16))
        grad_part.append(jnp.dot(projected, grad_pre[-1], preferred_element_type=f32).astype(bf16))
    grad_part = jnp.concatenate(grad_part, axis=1)
    partial_rows = sum(
        lax.dot_general(g, w, (((1,), (1,)), ((), ())), preferred_element_type=f32)
        for g, w in zip(grad_pre, (weight_a, weight_b))
    ).astype(bf16)

    landed = lax.all_to_all(grad_part.reshape(inner, outer * share, width), "fsdp", 0, 0, tiled=True)
    landed, partial_rows = lax.optimization_barrier((landed, partial_rows))
    token_rows = lax.psum_scatter(partial_rows, "tensor", scatter_dimension=0, tiled=True)
    inner_sum = jnp.sum(landed.astype(f32), axis=0)
    landed = lax.all_to_all(inner_sum.reshape(outer, share, width), "dp", 0, 0, tiled=True)
    landed, token_rows = lax.optimization_barrier((landed, token_rows))
    token_grad = lax.all_gather(token_rows, "tensor", axis=0, tiled=True)
    reduced = jnp.sum(landed, axis=0)

    token_count = tokens.shape[0] * outer * inner
    grad_low = reduced / float(token_count)
    new_first_moment = BETA_ONE * first_moment + (1.0 - BETA_ONE) * grad_low
    new_second_moment = BETA_TWO * second_moment + (1.0 - BETA_TWO) * grad_low * grad_low
    first_hat = new_first_moment / (1.0 - BETA_ONE**ADAM_STEP)
    second_hat = new_second_moment / (1.0 - BETA_TWO**ADAM_STEP)
    direction = (first_hat / (jnp.sqrt(second_hat) + EPSILON)).astype(bf16)
    column = spread(direction, "dp").reshape(outer * share, width)
    full_direction = spread(column, "fsdp").reshape(rank, width)
    update = jnp.dot(basis_perm, full_direction, preferred_element_type=f32)
    new_weight = (weight.astype(f32) - LEARN_RATE * update).astype(bf16)
    return (token_grad, new_weight, new_first_moment, new_second_moment)


def solution(mesh):
    in_specs = (
        P(("dp", "fsdp"), None),
        P(("dp", "fsdp"), "tensor"),
        P(("dp", "fsdp"), "tensor"),
        P(("dp", "fsdp"), None),
        P(("dp", "fsdp"), "tensor"),
        P(("dp", "fsdp"), "tensor"),
    )
    out_specs = (
        P(("dp", "fsdp"), None),
        P(("dp", "fsdp"), "tensor"),
        P(("dp", "fsdp"), "tensor"),
        P(("dp", "fsdp"), "tensor"),
    )
    return jax.shard_map(local, mesh=mesh, in_specs=in_specs, out_specs=out_specs, check_vma=False)
```

```python
import jax
import jax.numpy as jnp
from jax import lax
from jax.sharding import PartitionSpec as P

ADAM_STEP = 10


BETA_ONE = 0.9
BETA_TWO = 0.95
EPSILON = 1e-08
LEARN_RATE = 0.01
RING = 4
PAIR = 2


def silu_slope(preact):
    logistic = jax.nn.sigmoid(preact)
    return logistic * (1.0 + preact * (1.0 - logistic))


def spread(block, axis, groups=None):
    count = lax.axis_size(axis) if groups is None else len(groups[0])
    copies = jnp.broadcast_to(block[None], (count,) + block.shape)
    return lax.all_to_all(copies, axis, 0, 0, tiled=True, axis_index_groups=groups)


def ring_of_four(block, axis, step, place):
    count = lax.axis_size(axis)
    ahead = [((i + step) % count, i) for i in range(count)]
    behind = [(i, (i + step) % count) for i in range(count)]
    half = block.shape[0] // 2
    following = lax.ppermute(block, axis, ahead)
    preceding = lax.ppermute(block, axis, behind)
    far_front = lax.ppermute(following[:half], axis, ahead)
    far_back = lax.ppermute(preceding[half:], axis, behind)
    far = jnp.concatenate([far_front, far_back], axis=0)
    stacked = jnp.stack([block, following, far, preceding])
    return lambda wanted: lax.dynamic_index_in_dim(
        stacked, lax.rem(wanted - place + RING, RING), 0, keepdims=False
    )


def local(tokens, cotangent, weight, basis, first_moment, second_moment):
    f32, bf16 = jnp.float32, jnp.bfloat16
    outer, inner, quarters = lax.axis_size("dp"), lax.axis_size("fsdp"), lax.axis_size("tensor")
    rows, width = weight.shape
    rank = basis.shape[1]
    depth = outer * inner * rows
    share = rank // (outer * inner)
    far = outer // RING
    basis_perm = (
        basis.reshape(rows, far, RING, inner, share).transpose(0, 3, 2, 1, 4).reshape(rows, rank)
    )
    part = rank // quarters
    basis_part = lax.dynamic_slice_in_dim(basis_perm, lax.axis_index("tensor") * part, part, 1)

    pairs = [[PAIR * y + x for x in range(PAIR)] for y in range(RING)]
    columns = [[PAIR * y + x for y in range(RING)] for x in range(PAIR)]
    strides = [[i + RING * j for j in range(far)] for i in range(RING)]
    fours = [[RING * j + i for i in range(RING)] for j in range(far)]
    pair_rows = PAIR * rows
    half = width * 9 // 14
    plane = spread(weight[:, :half], "fsdp").reshape(inner * rows, half)
    weight_a = lax.all_gather(plane, "dp", axis=0, tiled=True)
    second = jnp.concatenate([weight[:, half:], basis_part], axis=1)
    plane, second = lax.optimization_barrier((plane, second))
    second = spread(second, "fsdp", pairs).reshape(pair_rows, width - half + part)
    strided = spread(second, "dp", strides)
    place = lax.rem(lax.axis_index("dp"), RING)
    pick = ring_of_four(strided, "dp", 1, place)
    line = jnp.stack([pick(r) for r in range(RING)], axis=1).reshape(outer, pair_rows, width - half + part)
    pick = ring_of_four(line, "fsdp", PAIR, lax.axis_index("fsdp") // PAIR)
    full_b = jnp.stack([pick(r) for r in range(RING)], axis=1).reshape(depth, width - half + part)
    weight_b, full_basis = full_b[:, : width - half], full_b[:, width - half :]

    projected_part = lax.dot_general(
        full_basis, tokens, (((0,), (1,)), ((), ())), preferred_element_type=f32
    ).astype(bf16)
    projected = spread(projected_part, "tensor").reshape(rank, tokens.shape[0])

    grad_pre, grad_part = [], []
    for side, wanted in ((weight_a, cotangent[:, :half]), (weight_b, cotangent[:, half:])):
        preact = jnp.dot(tokens, side, preferred_element_type=f32)
        grad_pre.append((wanted.astype(f32) * silu_slope(preact)).astype(bf16))
        grad_part.append(jnp.dot(projected, grad_pre[-1], preferred_element_type=f32).astype(bf16))
    grad_part = jnp.concatenate(grad_part, axis=1)
    partial_rows = sum(
        lax.dot_general(g, w, (((1,), (1,)), ((), ())), preferred_element_type=f32)
        for g, w in zip(grad_pre, (weight_a, weight_b))
    ).astype(bf16)

    landed = lax.all_to_all(grad_part.reshape(inner, outer * share, width), "fsdp", 0, 0, tiled=True)
    landed, partial_rows = lax.optimization_barrier((landed, partial_rows))
    token_rows = lax.psum_scatter(partial_rows, "tensor", scatter_dimension=0, tiled=True)
    inner_sum = jnp.sum(landed.astype(f32), axis=0)
    blocks = inner_sum.astype(bf16).reshape(RING, far * share, width)
    landed = lax.all_to_all(blocks, "dp", 0, 0, tiled=True, axis_index_groups=fours)
    blocks = jnp.sum(landed.astype(f32), axis=0).reshape(far, share, width)
    landed = lax.all_to_all(blocks, "dp", 0, 0, tiled=True, axis_index_groups=strides)
    reduced = jnp.sum(landed, axis=0)

    token_count = tokens.shape[0] * outer * inner
    grad_low = reduced / float(token_count)
    new_first_moment = BETA_ONE * first_moment + (1.0 - BETA_ONE) * grad_low
    new_second_moment = BETA_TWO * second_moment + (1.0 - BETA_TWO) * grad_low * grad_low
    first_hat = new_first_moment / (1.0 - BETA_ONE**ADAM_STEP)
    second_hat = new_second_moment / (1.0 - BETA_TWO**ADAM_STEP)
    direction = (first_hat / (jnp.sqrt(second_hat) + EPSILON)).astype(bf16)
    column = spread(direction, "dp", strides).reshape(far * share, width)
    column, token_rows = lax.optimization_barrier((column, token_rows))
    token_grad = lax.all_gather(token_rows, "tensor", axis=0, tiled=True)
    column = spread(column, "dp", fours).reshape(outer * share, width)
    full_direction = spread(column, "fsdp").reshape(rank, width)
    update = jnp.dot(basis_perm, full_direction, preferred_element_type=f32)
    new_weight = (weight.astype(f32) - LEARN_RATE * update).astype(bf16)
    return (token_grad, new_weight, new_first_moment, new_second_moment)


def solution(mesh):
    in_specs = (
        P(("dp", "fsdp"), None),
        P(("dp", "fsdp"), "tensor"),
        P(("dp", "fsdp"), "tensor"),
        P(("dp", "fsdp"), None),
        P(("dp", "fsdp"), "tensor"),
        P(("dp", "fsdp"), "tensor"),
    )
    out_specs = (
        P(("dp", "fsdp"), None),
        P(("dp", "fsdp"), "tensor"),
        P(("dp", "fsdp"), "tensor"),
        P(("dp", "fsdp"), "tensor"),
    )
    return jax.shard_map(local, mesh=mesh, in_specs=in_specs, out_specs=out_specs, check_vma=False)
```

```python
import jax
import jax.numpy as jnp
from jax import lax
from jax.sharding import PartitionSpec as P

ADAM_STEP = 10


BETA_ONE = 0.9
BETA_TWO = 0.95
EPSILON = 1e-08
LEARN_RATE = 0.01
RING = 4
PAIR = 2


def silu_slope(preact):
    logistic = jax.nn.sigmoid(preact)
    return logistic * (1.0 + preact * (1.0 - logistic))


def spread(block, axis, groups=None):
    count = lax.axis_size(axis) if groups is None else len(groups[0])
    copies = jnp.broadcast_to(block[None], (count,) + block.shape)
    return lax.all_to_all(copies, axis, 0, 0, tiled=True, axis_index_groups=groups)


def ring_of_four(block, axis, step, place):
    count = lax.axis_size(axis)
    ahead = [((i + step) % count, i) for i in range(count)]
    behind = [(i, (i + step) % count) for i in range(count)]
    half = block.shape[0] // 2
    following = lax.ppermute(block, axis, ahead)
    preceding = lax.ppermute(block, axis, behind)
    far_front = lax.ppermute(following[:half], axis, ahead)
    far_back = lax.ppermute(preceding[half:], axis, behind)
    far = jnp.concatenate([far_front, far_back], axis=0)
    stacked = jnp.stack([block, following, far, preceding])
    return lambda wanted: lax.dynamic_index_in_dim(
        stacked, lax.rem(wanted - place + RING, RING), 0, keepdims=False
    )


def local(tokens, cotangent, weight, basis, first_moment, second_moment):
    f32, bf16 = jnp.float32, jnp.bfloat16
    outer, inner, quarters = lax.axis_size("dp"), lax.axis_size("fsdp"), lax.axis_size("tensor")
    rows, width = weight.shape
    rank = basis.shape[1]
    depth = outer * inner * rows
    share = rank // (outer * inner)
    far = outer // RING
    basis_perm = (
        basis.reshape(rows, far, RING, inner, share).transpose(0, 3, 2, 1, 4).reshape(rows, rank)
    )
    part = rank // quarters
    basis_part = lax.dynamic_slice_in_dim(basis_perm, lax.axis_index("tensor") * part, part, 1)

    pairs = [[PAIR * y + x for x in range(PAIR)] for y in range(RING)]
    columns = [[PAIR * y + x for y in range(RING)] for x in range(PAIR)]
    strides = [[i + RING * j for j in range(far)] for i in range(RING)]
    fours = [[RING * j + i for i in range(RING)] for j in range(far)]
    pair_rows = PAIR * rows
    half = width * 9 // 14
    plane = spread(weight[:, :half], "fsdp").reshape(inner * rows, half)
    weight_a = lax.all_gather(plane, "dp", axis=0, tiled=True)
    second = jnp.concatenate([weight[:, half:], basis_part], axis=1)
    plane, second = lax.optimization_barrier((plane, second))
    second = spread(second, "fsdp", pairs).reshape(pair_rows, width - half + part)
    line = lax.all_gather(second, "dp", axis=0)
    pick = ring_of_four(line, "fsdp", PAIR, lax.axis_index("fsdp") // PAIR)
    full_b = jnp.stack([pick(r) for r in range(RING)], axis=1).reshape(depth, width - half + part)
    moments = jnp.stack([first_moment, second_moment])
    full_b, moments = lax.optimization_barrier((full_b, moments))
    moments = spread(moments, "dp", strides)
    weight_b, full_basis = full_b[:, : width - half], full_b[:, width - half :]

    projected_part = lax.dot_general(
        full_basis, tokens, (((0,), (1,)), ((), ())), preferred_element_type=f32
    ).astype(bf16)
    projected = spread(projected_part, "tensor").reshape(rank, tokens.shape[0])

    grad_pre, grad_part = [], []
    for side, wanted in ((weight_a, cotangent[:, :half]), (weight_b, cotangent[:, half:])):
        preact = jnp.dot(tokens, side, preferred_element_type=f32)
        grad_pre.append((wanted.astype(f32) * silu_slope(preact)).astype(bf16))
        grad_part.append(jnp.dot(projected, grad_pre[-1], preferred_element_type=f32).astype(bf16))
    grad_part, moments = lax.optimization_barrier((jnp.concatenate(grad_part, axis=1), moments))
    old_first, old_second = (moments[:, i].reshape(far * share, width) for i in range(2))
    partial_rows = sum(
        lax.dot_general(g, w, (((1,), (1,)), ((), ())), preferred_element_type=f32)
        for g, w in zip(grad_pre, (weight_a, weight_b))
    ).astype(bf16)

    landed = lax.all_to_all(grad_part.reshape(inner, outer * share, width), "fsdp", 0, 0, tiled=True)
    landed, partial_rows = lax.optimization_barrier((landed, partial_rows))
    token_rows = lax.psum_scatter(partial_rows, "tensor", scatter_dimension=0, tiled=True)
    inner_sum = jnp.sum(landed.astype(f32), axis=0)
    blocks = inner_sum.astype(bf16).reshape(RING, far * share, width)
    landed = lax.all_to_all(blocks, "dp", 0, 0, tiled=True, axis_index_groups=fours)
    blocks = jnp.sum(landed.astype(f32), axis=0).astype(bf16)
    landed = spread(blocks, "dp", strides)
    landed, token_rows = lax.optimization_barrier((landed, token_rows))
    token_grad = lax.all_gather(token_rows, "tensor", axis=0, tiled=True)
    reduced = jnp.sum(landed.astype(f32), axis=0)

    token_count = tokens.shape[0] * outer * inner
    grad_low = reduced / float(token_count)
    new_first = BETA_ONE * old_first + (1.0 - BETA_ONE) * grad_low
    new_second = BETA_TWO * old_second + (1.0 - BETA_TWO) * grad_low * grad_low
    first_hat = new_first / (1.0 - BETA_ONE**ADAM_STEP)
    second_hat = new_second / (1.0 - BETA_TWO**ADAM_STEP)
    direction = (first_hat / (jnp.sqrt(second_hat) + EPSILON)).astype(bf16)
    own = lax.axis_index("dp") // RING
    new_first_moment, new_second_moment = (
        lax.dynamic_index_in_dim(m.reshape(far, share, width), own, 0, keepdims=False)
        for m in (new_first, new_second)
    )
    column = spread(direction, "dp", fours).reshape(outer * share, width)
    full_direction = spread(column, "fsdp").reshape(rank, width)
    update = jnp.dot(basis_perm, full_direction, preferred_element_type=f32)
    new_weight = (weight.astype(f32) - LEARN_RATE * update).astype(bf16)
    return (token_grad, new_weight, new_first_moment, new_second_moment)


def solution(mesh):
    in_specs = (
        P(("dp", "fsdp"), None),
        P(("dp", "fsdp"), "tensor"),
        P(("dp", "fsdp"), "tensor"),
        P(("dp", "fsdp"), None),
        P(("dp", "fsdp"), "tensor"),
        P(("dp", "fsdp"), "tensor"),
    )
    out_specs = (
        P(("dp", "fsdp"), None),
        P(("dp", "fsdp"), "tensor"),
        P(("dp", "fsdp"), "tensor"),
        P(("dp", "fsdp"), "tensor"),
    )
    return jax.shard_map(local, mesh=mesh, in_specs=in_specs, out_specs=out_specs, check_vma=False)
```

```python
import jax
import jax.numpy as jnp
from jax import lax
from jax.sharding import PartitionSpec as P

ADAM_STEP = 10


BETA_ONE = 0.9
BETA_TWO = 0.95
EPSILON = 1e-08
LEARN_RATE = 0.01
RING = 4
PAIR = 2


def silu_slope(preact):
    logistic = jax.nn.sigmoid(preact)
    return logistic * (1.0 + preact * (1.0 - logistic))


def spread(block, axis, groups=None):
    count = lax.axis_size(axis) if groups is None else len(groups[0])
    copies = jnp.broadcast_to(block[None], (count,) + block.shape)
    return lax.all_to_all(copies, axis, 0, 0, tiled=True, axis_index_groups=groups)


def ring_permutes(axis, step):
    count = lax.axis_size(axis)
    ahead = [((i + step) % count, i) for i in range(count)]
    behind = [(i, (i + step) % count) for i in range(count)]
    return (lambda x: lax.ppermute(x, axis, ahead)), (lambda x: lax.ppermute(x, axis, behind))


def by_class(blocks, place):
    stacked = jnp.stack(blocks)
    return [
        lax.dynamic_index_in_dim(stacked, lax.rem(wanted - place + RING, RING), 0, keepdims=False)
        for wanted in range(RING)
    ]


def local(tokens, cotangent, weight, basis, first_moment, second_moment):
    f32, bf16 = jnp.float32, jnp.bfloat16
    outer, inner, quarters = lax.axis_size("dp"), lax.axis_size("fsdp"), lax.axis_size("tensor")
    rows, width = weight.shape
    rank = basis.shape[1]
    depth = outer * inner * rows
    share = rank // (outer * inner)
    far = outer // RING
    basis_perm = (
        basis.reshape(rows, far, RING, inner, share).transpose(0, 3, 2, 1, 4).reshape(rows, rank)
    )
    part = rank // quarters
    basis_part = lax.dynamic_slice_in_dim(basis_perm, lax.axis_index("tensor") * part, part, 1)

    pairs = [[PAIR * y + x for x in range(PAIR)] for y in range(RING)]
    columns = [[PAIR * y + x for y in range(RING)] for x in range(PAIR)]
    strides = [[i + RING * j for j in range(far)] for i in range(RING)]
    fours = [[RING * j + i for i in range(RING)] for j in range(far)]
    pair_rows = PAIR * rows
    half = width * 4 // 7
    first = jnp.concatenate([weight[:, :half], basis_part], axis=1)
    plane = spread(first, "fsdp").reshape(inner * rows, half + part)
    full_a = lax.all_gather(plane, "dp", axis=0, tiled=True)
    plane, second = lax.optimization_barrier((plane, weight[:, half:]))
    second = spread(second, "fsdp", pairs).reshape(pair_rows, width - half)
    line = lax.all_gather(second, "dp", axis=0)
    moments = jnp.stack([first_moment, second_moment])
    line, moments = lax.optimization_barrier((line, moments))
    from_ahead, from_behind = ring_permutes("fsdp", PAIR)
    ahead, behind = from_ahead(line), from_behind(line)
    moments = spread(moments, "dp", strides)
    ahead, behind, moments = lax.optimization_barrier((ahead, behind, moments))
    old_first, old_second = (moments[:, i].reshape(far * share, width) for i in range(2))
    across = from_ahead(ahead[: outer // 2]), from_behind(behind[outer // 2 :])

    def grad_of_preact(side, wanted):
        preact = jnp.dot(tokens, side, preferred_element_type=f32)
        return (wanted.astype(f32) * silu_slope(preact)).astype(bf16)

    weight_a, full_basis = full_a[:, :half], full_a[:, half:]
    projected_part = lax.dot_general(
        full_basis, tokens, (((0,), (1,)), ((), ())), preferred_element_type=f32
    ).astype(bf16)
    projected = spread(projected_part, "tensor").reshape(rank, tokens.shape[0])
    grad_pre_a = grad_of_preact(weight_a, cotangent[:, :half])
    across, grad_pre_a = lax.optimization_barrier((across, grad_pre_a))

    blocks = by_class([line, ahead, jnp.concatenate(across), behind], lax.axis_index("fsdp") // PAIR)
    weight_b = jnp.stack(blocks, axis=1).reshape(depth, width - half)
    grad_pre_b = grad_of_preact(weight_b, cotangent[:, half:])
    grad_part = jnp.concatenate(
        [
            jnp.dot(projected, g, preferred_element_type=f32).astype(bf16)
            for g in (grad_pre_a, grad_pre_b)
        ],
        axis=1,
    )
    partial_rows = sum(
        lax.dot_general(g, w, (((1,), (1,)), ((), ())), preferred_element_type=f32)
        for g, w in ((grad_pre_a, weight_a), (grad_pre_b, weight_b))
    ).astype(bf16)

    landed = lax.all_to_all(grad_part.reshape(inner, outer * share, width), "fsdp", 0, 0, tiled=True)
    landed, partial_rows = lax.optimization_barrier((landed, partial_rows))
    token_rows = lax.psum_scatter(partial_rows, "tensor", scatter_dimension=0, tiled=True)
    inner_sum = jnp.sum(landed.astype(f32), axis=0)
    blocks = inner_sum.astype(bf16).reshape(RING, far * share, width)
    landed = lax.all_to_all(blocks, "dp", 0, 0, tiled=True, axis_index_groups=fours)
    blocks = jnp.sum(landed.astype(f32), axis=0).astype(bf16)
    landed = spread(blocks, "dp", strides)
    landed, token_rows = lax.optimization_barrier((landed, token_rows))
    token_grad = lax.all_gather(token_rows, "tensor", axis=0, tiled=True)
    reduced = jnp.sum(landed.astype(f32), axis=0)

    token_count = tokens.shape[0] * outer * inner
    grad_low = reduced / float(token_count)
    new_first = BETA_ONE * old_first + (1.0 - BETA_ONE) * grad_low
    new_second = BETA_TWO * old_second + (1.0 - BETA_TWO) * grad_low * grad_low
    first_hat = new_first / (1.0 - BETA_ONE**ADAM_STEP)
    second_hat = new_second / (1.0 - BETA_TWO**ADAM_STEP)
    direction = (first_hat / (jnp.sqrt(second_hat) + EPSILON)).astype(bf16)
    own = lax.axis_index("dp") // RING
    new_first_moment, new_second_moment = (
        lax.dynamic_index_in_dim(m.reshape(far, share, width), own, 0, keepdims=False)
        for m in (new_first, new_second)
    )
    column = spread(direction, "dp", fours).reshape(outer * share, width)
    full_direction = spread(column, "fsdp").reshape(rank, width)
    update = jnp.dot(basis_perm, full_direction, preferred_element_type=f32)
    new_weight = (weight.astype(f32) - LEARN_RATE * update).astype(bf16)
    return (token_grad, new_weight, new_first_moment, new_second_moment)


def solution(mesh):
    in_specs = (
        P(("dp", "fsdp"), None),
        P(("dp", "fsdp"), "tensor"),
        P(("dp", "fsdp"), "tensor"),
        P(("dp", "fsdp"), None),
        P(("dp", "fsdp"), "tensor"),
        P(("dp", "fsdp"), "tensor"),
    )
    out_specs = (
        P(("dp", "fsdp"), None),
        P(("dp", "fsdp"), "tensor"),
        P(("dp", "fsdp"), "tensor"),
        P(("dp", "fsdp"), "tensor"),
    )
    return jax.shard_map(local, mesh=mesh, in_specs=in_specs, out_specs=out_specs, check_vma=False)
```

```python
import jax
import jax.numpy as jnp
from jax import lax
from jax.sharding import PartitionSpec as P

ADAM_STEP = 10


BETA_ONE = 0.9
BETA_TWO = 0.95
EPSILON = 1e-08
LEARN_RATE = 0.01
RING = 4
PAIR = 2


def silu_slope(preact):
    logistic = jax.nn.sigmoid(preact)
    return logistic * (1.0 + preact * (1.0 - logistic))


def spread(block, axis, groups=None):
    count = lax.axis_size(axis) if groups is None else len(groups[0])
    copies = jnp.broadcast_to(block[None], (count,) + block.shape)
    return lax.all_to_all(copies, axis, 0, 0, tiled=True, axis_index_groups=groups)


def ring_permutes(axis, step):
    count = lax.axis_size(axis)
    ahead = [((i + step) % count, i) for i in range(count)]
    behind = [(i, (i + step) % count) for i in range(count)]
    return (lambda x: lax.ppermute(x, axis, ahead)), (lambda x: lax.ppermute(x, axis, behind))


def by_class(blocks, place):
    stacked = jnp.stack(blocks)
    return [
        lax.dynamic_index_in_dim(stacked, lax.rem(wanted - place + RING, RING), 0, keepdims=False)
        for wanted in range(RING)
    ]


def local(tokens, cotangent, weight, basis, first_moment, second_moment):
    f32, bf16 = jnp.float32, jnp.bfloat16
    outer, inner, quarters = lax.axis_size("dp"), lax.axis_size("fsdp"), lax.axis_size("tensor")
    rows, width = weight.shape
    rank = basis.shape[1]
    depth = outer * inner * rows
    share = rank // (outer * inner)
    far = outer // RING
    basis_perm = (
        basis.reshape(rows, far, RING, inner, share).transpose(0, 3, 2, 1, 4).reshape(rows, rank)
    )
    part = rank // quarters
    basis_part = lax.dynamic_slice_in_dim(basis_perm, lax.axis_index("tensor") * part, part, 1)

    pairs = [[PAIR * y + x for x in range(PAIR)] for y in range(RING)]
    columns = [[PAIR * y + x for y in range(RING)] for x in range(PAIR)]
    strides = [[i + RING * j for j in range(far)] for i in range(RING)]
    fours = [[RING * j + i for i in range(RING)] for j in range(far)]
    pair_rows = PAIR * rows
    half = width * 4 // 7
    first = jnp.concatenate([weight[:, :half], basis_part], axis=1)
    plane = spread(first, "fsdp").reshape(inner * rows, half + part)
    full_a = lax.all_gather(plane, "dp", axis=0, tiled=True)
    plane, second = lax.optimization_barrier((plane, weight[:, half:]))
    second = spread(second, "fsdp", pairs).reshape(pair_rows, width - half)
    line = lax.all_gather(second, "dp", axis=0)
    moments = jnp.stack([first_moment, second_moment])
    line, moments = lax.optimization_barrier((line, moments))
    from_ahead, from_behind = ring_permutes("fsdp", PAIR)
    ahead, behind = from_ahead(line), from_behind(line)
    moments = spread(moments, "dp", strides)
    across = from_ahead(ahead[: outer // 2]), from_behind(behind[outer // 2 :])

    def grad_of_preact(side, wanted):
        preact = jnp.dot(tokens, side, preferred_element_type=f32)
        return (wanted.astype(f32) * silu_slope(preact)).astype(bf16)

    weight_a, full_basis = full_a[:, :half], full_a[:, half:]
    projected_part = lax.dot_general(
        full_basis, tokens, (((0,), (1,)), ((), ())), preferred_element_type=f32
    ).astype(bf16)
    projected = spread(projected_part, "tensor").reshape(rank, tokens.shape[0])
    grad_pre_a = grad_of_preact(weight_a, cotangent[:, :half])
    across, moments = lax.optimization_barrier((across, moments))
    old_first, old_second = (moments[:, i].reshape(far * share, width) for i in range(2))

    blocks = by_class([line, ahead, jnp.concatenate(across), behind], lax.axis_index("fsdp") // PAIR)
    weight_b = jnp.stack(blocks, axis=1).reshape(depth, width - half)
    grad_pre_b = grad_of_preact(weight_b, cotangent[:, half:])
    grad_part = jnp.concatenate(
        [
            jnp.dot(projected, g, preferred_element_type=f32).astype(bf16)
            for g in (grad_pre_a, grad_pre_b)
        ],
        axis=1,
    )
    grad_part, grad_pre_a, grad_pre_b = lax.optimization_barrier(
        (grad_part, grad_pre_a, grad_pre_b)
    )
    partial_rows = sum(
        lax.dot_general(g, w, (((1,), (1,)), ((), ())), preferred_element_type=f32)
        for g, w in ((grad_pre_a, weight_a), (grad_pre_b, weight_b))
    ).astype(bf16)

    landed = lax.all_to_all(grad_part.reshape(inner, outer * share, width), "fsdp", 0, 0, tiled=True)
    landed, _ = lax.optimization_barrier((landed, partial_rows))
    token_rows = lax.psum_scatter(partial_rows, "tensor", scatter_dimension=0, tiled=True)
    inner_sum = jnp.sum(landed.astype(f32), axis=0)
    blocks = inner_sum.astype(bf16).reshape(RING, far * share, width)
    landed = lax.all_to_all(blocks, "dp", 0, 0, tiled=True, axis_index_groups=fours)
    landed, token_rows = lax.optimization_barrier((landed, token_rows))
    token_grad = lax.all_gather(token_rows, "tensor", axis=0, tiled=True)
    blocks = jnp.sum(landed.astype(f32), axis=0).astype(bf16)
    landed = spread(blocks, "dp", strides)
    reduced = jnp.sum(landed.astype(f32), axis=0)

    token_count = tokens.shape[0] * outer * inner
    grad_low = reduced / float(token_count)
    new_first = BETA_ONE * old_first + (1.0 - BETA_ONE) * grad_low
    new_second = BETA_TWO * old_second + (1.0 - BETA_TWO) * grad_low * grad_low
    first_hat = new_first / (1.0 - BETA_ONE**ADAM_STEP)
    second_hat = new_second / (1.0 - BETA_TWO**ADAM_STEP)
    direction = (first_hat / (jnp.sqrt(second_hat) + EPSILON)).astype(bf16)
    own = lax.axis_index("dp") // RING
    new_first_moment, new_second_moment = (
        lax.dynamic_index_in_dim(m.reshape(far, share, width), own, 0, keepdims=False)
        for m in (new_first, new_second)
    )
    column = spread(direction, "dp", fours).reshape(outer * share, width)
    full_direction = spread(column, "fsdp").reshape(rank, width)
    update = jnp.dot(basis_perm, full_direction, preferred_element_type=f32)
    new_weight = (weight.astype(f32) - LEARN_RATE * update).astype(bf16)
    return (token_grad, new_weight, new_first_moment, new_second_moment)


def solution(mesh):
    in_specs = (
        P(("dp", "fsdp"), None),
        P(("dp", "fsdp"), "tensor"),
        P(("dp", "fsdp"), "tensor"),
        P(("dp", "fsdp"), None),
        P(("dp", "fsdp"), "tensor"),
        P(("dp", "fsdp"), "tensor"),
    )
    out_specs = (
        P(("dp", "fsdp"), None),
        P(("dp", "fsdp"), "tensor"),
        P(("dp", "fsdp"), "tensor"),
        P(("dp", "fsdp"), "tensor"),
    )
    return jax.shard_map(local, mesh=mesh, in_specs=in_specs, out_specs=out_specs, check_vma=False)
```

```python
import jax
import jax.numpy as jnp
from jax import lax
from jax.sharding import PartitionSpec as P

ADAM_STEP = 10


BETA_ONE = 0.9
BETA_TWO = 0.95
EPSILON = 1e-08
LEARN_RATE = 0.01
RING = 4
PAIR = 2


def silu_slope(preact):
    logistic = jax.nn.sigmoid(preact)
    return logistic * (1.0 + preact * (1.0 - logistic))


def spread(block, axis, groups=None):
    count = lax.axis_size(axis) if groups is None else len(groups[0])
    copies = jnp.broadcast_to(block[None], (count,) + block.shape)
    return lax.all_to_all(copies, axis, 0, 0, tiled=True, axis_index_groups=groups)


def ring_permutes(axis, step):
    count = lax.axis_size(axis)
    ahead = [((i + step) % count, i) for i in range(count)]
    behind = [(i, (i + step) % count) for i in range(count)]
    return (lambda x: lax.ppermute(x, axis, ahead)), (lambda x: lax.ppermute(x, axis, behind))


def by_class(blocks, place):
    count = len(blocks)
    stacked = jnp.stack(blocks)
    return [
        lax.dynamic_index_in_dim(stacked, lax.rem(wanted - place + count, count), 0, keepdims=False)
        for wanted in range(count)
    ]


def local(tokens, cotangent, weight, basis, first_moment, second_moment):
    f32, bf16 = jnp.float32, jnp.bfloat16
    outer, inner, quarters = lax.axis_size("dp"), lax.axis_size("fsdp"), lax.axis_size("tensor")
    rows, width = weight.shape
    rank = basis.shape[1]
    depth = outer * inner * rows
    share = rank // (outer * inner)
    far = outer // RING
    basis_perm = (
        basis.reshape(rows, far, RING, inner, share).transpose(0, 3, 2, 1, 4).reshape(rows, rank)
    )
    part = rank // quarters
    basis_part = lax.dynamic_slice_in_dim(basis_perm, lax.axis_index("tensor") * part, part, 1)

    pairs = [[PAIR * y + x for x in range(PAIR)] for y in range(RING)]
    columns = [[PAIR * y + x for y in range(RING)] for x in range(PAIR)]
    strides = [[i + RING * j for j in range(far)] for i in range(RING)]
    fours = [[RING * j + i for i in range(RING)] for j in range(far)]
    pair_rows = PAIR * rows
    half = width * 9 // 14
    first = jnp.concatenate([weight[:, :half], basis_part], axis=1)
    plane = spread(first, "fsdp").reshape(inner * rows, half + part)
    full_a = lax.all_gather(plane, "dp", axis=0, tiled=True)
    plane, second = lax.optimization_barrier((plane, weight[:, half:]))
    second = spread(second, "fsdp", pairs).reshape(pair_rows, width - half)
    line = lax.all_gather(second, "dp", axis=0)
    moments = jnp.stack([first_moment, second_moment])
    line, moments = lax.optimization_barrier((line, moments))
    from_ahead, from_behind = ring_permutes("fsdp", PAIR)
    ahead, behind = from_ahead(line), from_behind(line)
    carried = [moments] + [ring_permutes("dp", RING * j)[0](moments) for j in range(1, far)]
    ahead, behind = lax.optimization_barrier((ahead, behind))
    across = from_ahead(ahead[: outer // 2]), from_behind(behind[outer // 2 :])

    def grad_of_preact(side, wanted):
        preact = jnp.dot(tokens, side, preferred_element_type=f32)
        return (wanted.astype(f32) * silu_slope(preact)).astype(bf16)

    weight_a, full_basis = full_a[:, :half], full_a[:, half:]
    projected_part = lax.dot_general(
        full_basis, tokens, (((0,), (1,)), ((), ())), preferred_element_type=f32
    ).astype(bf16)
    projected = spread(projected_part, "tensor").reshape(rank, tokens.shape[0])
    grad_pre_a = grad_of_preact(weight_a, cotangent[:, :half])
    across, carried = lax.optimization_barrier((across, carried))
    moments = jnp.stack(by_class(carried, lax.axis_index("dp") // RING))

    blocks = by_class([line, ahead, jnp.concatenate(across), behind], lax.axis_index("fsdp") // PAIR)
    weight_b = jnp.stack(blocks, axis=1).reshape(depth, width - half)
    grad_pre_b = grad_of_preact(weight_b, cotangent[:, half:])
    grad_part = jnp.concatenate(
        [
            jnp.dot(projected, g, preferred_element_type=f32).astype(bf16)
            for g in (grad_pre_a, grad_pre_b)
        ],
        axis=1,
    )
    partial_rows = sum(
        lax.dot_general(g, w, (((1,), (1,)), ((), ())), preferred_element_type=f32)
        for g, w in ((grad_pre_a, weight_a), (grad_pre_b, weight_b))
    ).astype(bf16)

    landed = lax.all_to_all(grad_part.reshape(inner, outer * share, width), "fsdp", 0, 0, tiled=True)
    landed, partial_rows = lax.optimization_barrier((landed, partial_rows))
    token_rows = lax.psum_scatter(partial_rows, "tensor", scatter_dimension=0, tiled=True)
    inner_sum = jnp.sum(landed.astype(f32), axis=0)
    blocks = inner_sum.astype(bf16).reshape(RING, far * share, width)
    landed = lax.all_to_all(blocks, "dp", 0, 0, tiled=True, axis_index_groups=fours)
    blocks = jnp.sum(landed.astype(f32), axis=0).astype(bf16)
    landed = spread(blocks, "dp", strides)
    old_first, old_second = (moments[:, i].reshape(far * share, width) for i in range(2))
    old_first, token_rows = lax.optimization_barrier((BETA_ONE * old_first, token_rows))
    token_grad = lax.all_gather(token_rows, "tensor", axis=0, tiled=True)
    reduced = jnp.sum(landed.astype(f32), axis=0)

    token_count = tokens.shape[0] * outer * inner
    grad_low = reduced / float(token_count)
    new_first = old_first + (1.0 - BETA_ONE) * grad_low
    new_second = BETA_TWO * old_second + (1.0 - BETA_TWO) * grad_low * grad_low
    first_hat = new_first / (1.0 - BETA_ONE**ADAM_STEP)
    second_hat = new_second / (1.0 - BETA_TWO**ADAM_STEP)
    direction = (first_hat / (jnp.sqrt(second_hat) + EPSILON)).astype(bf16)
    own = lax.axis_index("dp") // RING
    new_first_moment, new_second_moment = (
        lax.dynamic_index_in_dim(m.reshape(far, share, width), own, 0, keepdims=False)
        for m in (new_first, new_second)
    )
    column = spread(direction, "dp", fours).reshape(outer * share, width)
    full_direction = spread(column, "fsdp").reshape(rank, width)
    update = jnp.dot(basis_perm, full_direction, preferred_element_type=f32)
    new_weight = (weight.astype(f32) - LEARN_RATE * update).astype(bf16)
    return (token_grad, new_weight, new_first_moment, new_second_moment)


def solution(mesh):
    in_specs = (
        P(("dp", "fsdp"), None),
        P(("dp", "fsdp"), "tensor"),
        P(("dp", "fsdp"), "tensor"),
        P(("dp", "fsdp"), None),
        P(("dp", "fsdp"), "tensor"),
        P(("dp", "fsdp"), "tensor"),
    )
    out_specs = (
        P(("dp", "fsdp"), None),
        P(("dp", "fsdp"), "tensor"),
        P(("dp", "fsdp"), "tensor"),
        P(("dp", "fsdp"), "tensor"),
    )
    return jax.shard_map(local, mesh=mesh, in_specs=in_specs, out_specs=out_specs, check_vma=False)
```

```python
import jax
import jax.numpy as jnp
from jax import lax
from jax.sharding import PartitionSpec as P

ADAM_STEP = 10


BETA_ONE = 0.9
BETA_TWO = 0.95
EPSILON = 1e-08
LEARN_RATE = 0.01
RING = 4
LANES = 128
PAIR = 2


def silu_slope(preact):
    logistic = jax.nn.sigmoid(preact)
    return logistic * (1.0 + preact * (1.0 - logistic))


def spread(block, axis, groups=None):
    count = lax.axis_size(axis) if groups is None else len(groups[0])
    copies = jnp.broadcast_to(block[None], (count,) + block.shape)
    return lax.all_to_all(copies, axis, 0, 0, tiled=True, axis_index_groups=groups)


def ring_permutes(axis, step):
    count = lax.axis_size(axis)
    ahead = [((i + step) % count, i) for i in range(count)]
    behind = [(i, (i + step) % count) for i in range(count)]
    return (lambda x: lax.ppermute(x, axis, ahead)), (lambda x: lax.ppermute(x, axis, behind))


def by_class(blocks, place):
    count = len(blocks)
    stacked = jnp.stack(blocks)
    return [
        lax.dynamic_index_in_dim(stacked, lax.rem(wanted - place + count, count), 0, keepdims=False)
        for wanted in range(count)
    ]


def local(tokens, cotangent, weight, basis, first_moment, second_moment):
    f32, bf16 = jnp.float32, jnp.bfloat16
    outer, inner, quarters = lax.axis_size("dp"), lax.axis_size("fsdp"), lax.axis_size("tensor")
    rows, width = weight.shape
    rank = basis.shape[1]
    depth = outer * inner * rows
    share = rank // (outer * inner)
    far = outer // RING
    basis_perm = (
        basis.reshape(rows, far, RING, inner, share).transpose(0, 3, 2, 1, 4).reshape(rows, rank)
    )
    part = rank // quarters
    basis_part = lax.dynamic_slice_in_dim(basis_perm, lax.axis_index("tensor") * part, part, 1)

    pairs = [[PAIR * y + x for x in range(PAIR)] for y in range(RING)]
    columns = [[PAIR * y + x for y in range(RING)] for x in range(PAIR)]
    strides = [[i + RING * j for j in range(far)] for i in range(RING)]
    fours = [[RING * j + i for i in range(RING)] for j in range(far)]
    pair_rows = PAIR * rows
    half = width * 9 // 14
    first = jnp.concatenate([weight[:, :half], basis_part], axis=1)
    plane = spread(first, "fsdp").reshape(inner * rows, half + part)
    spare = -(half + part) % LANES
    moments = jnp.concatenate([first_moment, second_moment]).astype(bf16).reshape(-1, spare)
    moments = jnp.pad(moments, ((0, inner * rows - moments.shape[0]), (0, 0)))
    plane = jnp.concatenate([plane, moments], axis=1)
    full_a = lax.all_gather(plane, "dp", axis=0, tiled=True)
    plane, second = lax.optimization_barrier((plane, weight[:, half:]))
    second = spread(second, "fsdp", pairs).reshape(pair_rows, width - half)
    line = lax.all_gather(second, "dp", axis=0)
    from_ahead, from_behind = ring_permutes("fsdp", PAIR)
    ahead, behind = from_ahead(line), from_behind(line)
    across = from_ahead(ahead[: outer // 2]), from_behind(behind[outer // 2 :])

    def grad_of_preact(side, wanted):
        preact = jnp.dot(tokens, side, preferred_element_type=f32)
        return (wanted.astype(f32) * silu_slope(preact)).astype(bf16)

    weight_a, full_basis = full_a[:, :half], full_a[:, half : half + part]
    projected_part = lax.dot_general(
        full_basis, tokens, (((0,), (1,)), ((), ())), preferred_element_type=f32
    ).astype(bf16)
    projected = spread(projected_part, "tensor").reshape(rank, tokens.shape[0])
    grad_pre_a = grad_of_preact(weight_a, cotangent[:, :half])
    blocks = by_class([line, ahead, jnp.concatenate(across), behind], lax.axis_index("fsdp") // PAIR)
    weight_b = jnp.stack(blocks, axis=1).reshape(depth, width - half)
    grad_pre_b = grad_of_preact(weight_b, cotangent[:, half:])
    grad_part = jnp.concatenate(
        [
            jnp.dot(projected, g, preferred_element_type=f32).astype(bf16)
            for g in (grad_pre_a, grad_pre_b)
        ],
        axis=1,
    )
    partial_rows = sum(
        lax.dot_general(g, w, (((1,), (1,)), ((), ())), preferred_element_type=f32)
        for g, w in ((grad_pre_a, weight_a), (grad_pre_b, weight_b))
    ).astype(bf16)

    landed = lax.all_to_all(grad_part.reshape(inner, outer * share, width), "fsdp", 0, 0, tiled=True)
    landed, partial_rows = lax.optimization_barrier((landed, partial_rows))
    token_rows = lax.psum_scatter(partial_rows, "tensor", scatter_dimension=0, tiled=True)
    inner_sum = jnp.sum(landed.astype(f32), axis=0)
    blocks = inner_sum.astype(bf16).reshape(RING, far * share, width)
    landed = lax.all_to_all(blocks, "dp", 0, 0, tiled=True, axis_index_groups=fours)
    blocks = jnp.sum(landed.astype(f32), axis=0).astype(bf16)
    landed = spread(blocks, "dp", strides)
    old = full_a[:, half + part :].reshape(far, RING, inner * rows, spare)
    old = lax.dynamic_index_in_dim(old, lax.rem(lax.axis_index("dp"), RING), 1, keepdims=False)
    old = old[:, : 2 * share * width // spare].reshape(far, 2, share, width).astype(f32)
    old_first, old_second = old[:, 0], old[:, 1]
    old_first, token_rows = lax.optimization_barrier((BETA_ONE * old_first, token_rows))
    token_grad = lax.all_gather(token_rows, "tensor", axis=0, tiled=True)
    reduced = jnp.sum(landed.astype(f32), axis=0).reshape(far, share, width)

    token_count = tokens.shape[0] * outer * inner
    grad_low = reduced / float(token_count)
    new_first = old_first + (1.0 - BETA_ONE) * grad_low
    new_second = BETA_TWO * old_second + (1.0 - BETA_TWO) * grad_low * grad_low
    first_hat = new_first / (1.0 - BETA_ONE**ADAM_STEP)
    second_hat = new_second / (1.0 - BETA_TWO**ADAM_STEP)
    direction = (first_hat / (jnp.sqrt(second_hat) + EPSILON)).astype(bf16)
    own = lax.dynamic_index_in_dim(grad_low, lax.axis_index("dp") // RING, 0, keepdims=False)
    new_first_moment = BETA_ONE * first_moment + (1.0 - BETA_ONE) * own
    new_second_moment = BETA_TWO * second_moment + (1.0 - BETA_TWO) * own * own
    column = spread(direction.reshape(far * share, width), "fsdp", pairs)
    column = spread(column.reshape(PAIR * far * share, width), "dp", fours)
    column = column.reshape(PAIR * outer * share, width)
    full_direction = spread(column, "fsdp", columns).reshape(rank, width)
    basis_last = (
        basis.reshape(rows, far, RING, RING, PAIR, share)
        .transpose(0, 3, 2, 4, 1, 5)
        .reshape(rows, rank)
    )
    update = jnp.dot(basis_last, full_direction, preferred_element_type=f32)
    new_weight = (weight.astype(f32) - LEARN_RATE * update).astype(bf16)
    return (token_grad, new_weight, new_first_moment, new_second_moment)


def solution(mesh):
    in_specs = (
        P(("dp", "fsdp"), None),
        P(("dp", "fsdp"), "tensor"),
        P(("dp", "fsdp"), "tensor"),
        P(("dp", "fsdp"), None),
        P(("dp", "fsdp"), "tensor"),
        P(("dp", "fsdp"), "tensor"),
    )
    out_specs = (
        P(("dp", "fsdp"), None),
        P(("dp", "fsdp"), "tensor"),
        P(("dp", "fsdp"), "tensor"),
        P(("dp", "fsdp"), "tensor"),
    )
    return jax.shard_map(local, mesh=mesh, in_specs=in_specs, out_specs=out_specs, check_vma=False)
```

```python
import jax
import jax.numpy as jnp
from jax import lax
from jax.experimental import pallas as pl
from jax.experimental.pallas import tpu as pltpu
from jax.sharding import PartitionSpec as P

ADAM_STEP = 10


BETA_ONE = 0.9
BETA_TWO = 0.95
EPSILON = 1e-08
LEARN_RATE = 0.01
RING = 4
LANES = 128
PAIR = 2


def silu_slope(preact):
    logistic = jax.nn.sigmoid(preact)
    return logistic * (1.0 + preact * (1.0 - logistic))


def slope_kernel(tokens_ref, weight_ref, cotangent_ref, out_ref):
    preact = jnp.dot(tokens_ref[...], weight_ref[...], preferred_element_type=jnp.float32)
    wanted = cotangent_ref[...].astype(jnp.float32)
    out_ref[...] = (wanted * silu_slope(preact)).astype(out_ref.dtype)


def grad_of_first(tokens, weight, cotangent, width):
    count, depth = tokens.shape
    block = 3 * LANES
    return pl.pallas_call(
        slope_kernel,
        grid=(width // block,),
        in_specs=[
            pl.BlockSpec((count, depth), lambda i: (0, 0)),
            pl.BlockSpec((depth, block), lambda i: (0, i)),
            pl.BlockSpec((count, block), lambda i: (0, i)),
        ],
        out_specs=pl.BlockSpec((count, block), lambda i: (0, i)),
        out_shape=jax.ShapeDtypeStruct((count, width), jnp.bfloat16),
        compiler_params=pltpu.CompilerParams(vmem_limit_bytes=16 * 1024 * 1024),
        cost_estimate=pl.CostEstimate(
            flops=2 * count * depth * width,
            bytes_accessed=2 * (depth * width + count * (depth + 2 * width)),
            transcendentals=count * width,
        ),
    )(tokens, weight, cotangent)


def spread(block, axis, groups=None):
    count = lax.axis_size(axis) if groups is None else len(groups[0])
    copies = jnp.broadcast_to(block[None], (count,) + block.shape)
    return lax.all_to_all(copies, axis, 0, 0, tiled=True, axis_index_groups=groups)


def ring_permutes(axis, step):
    count = lax.axis_size(axis)
    ahead = [((i + step) % count, i) for i in range(count)]
    behind = [(i, (i + step) % count) for i in range(count)]
    return (lambda x: lax.ppermute(x, axis, ahead)), (lambda x: lax.ppermute(x, axis, behind))


def by_class(blocks, place):
    count = len(blocks)
    stacked = jnp.stack(blocks)
    return [
        lax.dynamic_index_in_dim(stacked, lax.rem(wanted - place + count, count), 0, keepdims=False)
        for wanted in range(count)
    ]


def local(tokens, cotangent, weight, basis, first_moment, second_moment):
    f32, bf16 = jnp.float32, jnp.bfloat16
    outer, inner, quarters = lax.axis_size("dp"), lax.axis_size("fsdp"), lax.axis_size("tensor")
    rows, width = weight.shape
    rank = basis.shape[1]
    depth = outer * inner * rows
    share = rank // (outer * inner)
    far = outer // RING
    basis_perm = (
        basis.reshape(rows, far, RING, inner, share).transpose(0, 3, 2, 1, 4).reshape(rows, rank)
    )
    part = rank // quarters
    basis_part = lax.dynamic_slice_in_dim(basis_perm, lax.axis_index("tensor") * part, part, 1)

    pairs = [[PAIR * y + x for x in range(PAIR)] for y in range(RING)]
    columns = [[PAIR * y + x for y in range(RING)] for x in range(PAIR)]
    strides = [[i + RING * j for j in range(far)] for i in range(RING)]
    fours = [[RING * j + i for i in range(RING)] for j in range(far)]
    pair_rows = PAIR * rows
    half = width * 9 // 14
    first = jnp.concatenate([weight[:, :half], basis_part], axis=1)
    plane = spread(first, "fsdp").reshape(inner * rows, half + part)
    spare = -(half + part) % LANES
    moments = jnp.concatenate([first_moment, second_moment]).astype(bf16).reshape(-1, spare)
    moments = jnp.pad(moments, ((0, inner * rows - moments.shape[0]), (0, 0)))
    plane = jnp.concatenate([plane, moments], axis=1)
    full_a = lax.all_gather(plane, "dp", axis=0, tiled=True)
    plane, second = lax.optimization_barrier((plane, weight[:, half:]))
    second = spread(second, "fsdp", pairs).reshape(pair_rows, width - half)
    line = lax.all_gather(second, "dp", axis=0)
    from_ahead, from_behind = ring_permutes("fsdp", PAIR)
    ahead, behind = from_ahead(line), from_behind(line)
    across = from_ahead(ahead[: outer // 2]), from_behind(behind[outer // 2 :])

    def grad_of_preact(side, wanted):
        preact = jnp.dot(tokens, side, preferred_element_type=f32)
        return (wanted.astype(f32) * silu_slope(preact)).astype(bf16)

    weight_a, full_basis = full_a[:, :half], full_a[:, half : half + part]
    projected_part = lax.dot_general(
        full_basis, tokens, (((0,), (1,)), ((), ())), preferred_element_type=f32
    ).astype(bf16)
    projected = spread(projected_part, "tensor").reshape(rank, tokens.shape[0])
    grad_pre_a = grad_of_first(tokens, full_a, cotangent, half)
    blocks = by_class([line, ahead, jnp.concatenate(across), behind], lax.axis_index("fsdp") // PAIR)
    weight_b = jnp.stack(blocks, axis=1).reshape(depth, width - half)
    grad_pre_b = grad_of_preact(weight_b, cotangent[:, half:])
    grad_part = jnp.concatenate(
        [
            jnp.dot(projected, g, preferred_element_type=f32).astype(bf16)
            for g in (grad_pre_a, grad_pre_b)
        ],
        axis=1,
    )
    partial_rows = sum(
        lax.dot_general(g, w, (((1,), (1,)), ((), ())), preferred_element_type=f32)
        for g, w in ((grad_pre_a, weight_a), (grad_pre_b, weight_b))
    ).astype(bf16)

    landed = lax.all_to_all(grad_part.reshape(inner, outer * share, width), "fsdp", 0, 0, tiled=True)
    landed, partial_rows = lax.optimization_barrier((landed, partial_rows))
    token_rows = lax.psum_scatter(partial_rows, "tensor", scatter_dimension=0, tiled=True)
    inner_sum = jnp.sum(landed.astype(f32), axis=0)
    blocks = inner_sum.astype(bf16).reshape(RING, far * share, width)
    landed = lax.all_to_all(blocks, "dp", 0, 0, tiled=True, axis_index_groups=fours)
    blocks = jnp.sum(landed.astype(f32), axis=0).astype(bf16)
    landed = spread(blocks, "dp", strides)
    old = full_a[:, half + part :].reshape(far, RING, inner * rows, spare)
    old = lax.dynamic_index_in_dim(old, lax.rem(lax.axis_index("dp"), RING), 1, keepdims=False)
    old = old[:, : 2 * share * width // spare].reshape(far, 2, share, width).astype(f32)
    old_first, old_second = old[:, 0], old[:, 1]
    old_first, token_rows = lax.optimization_barrier((BETA_ONE * old_first, token_rows))
    token_grad = lax.all_gather(token_rows, "tensor", axis=0, tiled=True)
    reduced = jnp.sum(landed.astype(f32), axis=0).reshape(far, share, width)

    token_count = tokens.shape[0] * outer * inner
    grad_low = reduced / float(token_count)
    new_first = old_first + (1.0 - BETA_ONE) * grad_low
    new_second = BETA_TWO * old_second + (1.0 - BETA_TWO) * grad_low * grad_low
    first_hat = new_first / (1.0 - BETA_ONE**ADAM_STEP)
    second_hat = new_second / (1.0 - BETA_TWO**ADAM_STEP)
    direction = (first_hat / (jnp.sqrt(second_hat) + EPSILON)).astype(bf16)
    own = lax.dynamic_index_in_dim(grad_low, lax.axis_index("dp") // RING, 0, keepdims=False)
    new_first_moment = BETA_ONE * first_moment + (1.0 - BETA_ONE) * own
    new_second_moment = BETA_TWO * second_moment + (1.0 - BETA_TWO) * own * own
    column = spread(direction.reshape(far * share, width), "fsdp", pairs)
    column = spread(column.reshape(PAIR * far * share, width), "dp", fours)
    column = column.reshape(PAIR * outer * share, width)
    full_direction = spread(column, "fsdp", columns).reshape(rank, width)
    token_grad = token_grad * lax.optimization_barrier(jnp.ones((), bf16))
    full_direction, token_grad = lax.optimization_barrier((full_direction, token_grad))
    basis_last = (
        basis.reshape(rows, far, RING, RING, PAIR, share)
        .transpose(0, 3, 2, 4, 1, 5)
        .reshape(rows, rank)
    )
    update = jnp.dot(basis_last, full_direction, preferred_element_type=f32)
    new_weight = (weight.astype(f32) - LEARN_RATE * update).astype(bf16)
    return (token_grad, new_weight, new_first_moment, new_second_moment)


def solution(mesh):
    in_specs = (
        P(("dp", "fsdp"), None),
        P(("dp", "fsdp"), "tensor"),
        P(("dp", "fsdp"), "tensor"),
        P(("dp", "fsdp"), None),
        P(("dp", "fsdp"), "tensor"),
        P(("dp", "fsdp"), "tensor"),
    )
    out_specs = (
        P(("dp", "fsdp"), None),
        P(("dp", "fsdp"), "tensor"),
        P(("dp", "fsdp"), "tensor"),
        P(("dp", "fsdp"), "tensor"),
    )
    return jax.shard_map(local, mesh=mesh, in_specs=in_specs, out_specs=out_specs, check_vma=False)
```

```python
import jax
import jax.numpy as jnp
from jax import lax
from jax.experimental import pallas as pl
from jax.experimental.pallas import tpu as pltpu
from jax.sharding import PartitionSpec as P

ADAM_STEP = 10


BETA_ONE = 0.9
BETA_TWO = 0.95
EPSILON = 1e-08
LEARN_RATE = 0.01
RING = 4
LANES = 128
PAIR = 2


def silu_slope(preact):
    logistic = jax.nn.sigmoid(preact)
    return logistic * (1.0 + preact * (1.0 - logistic))


def slope_kernel(tokens_ref, weight_ref, cotangent_ref, out_ref):
    preact = jnp.dot(tokens_ref[...], weight_ref[...], preferred_element_type=jnp.float32)
    wanted = cotangent_ref[...].astype(jnp.float32)
    out_ref[...] = (wanted * silu_slope(preact)).astype(out_ref.dtype)


def grad_of_first(tokens, weight, cotangent, width):
    count, depth = tokens.shape
    block = 3 * LANES
    return pl.pallas_call(
        slope_kernel,
        grid=(width // block,),
        in_specs=[
            pl.BlockSpec((count, depth), lambda i: (0, 0)),
            pl.BlockSpec((depth, block), lambda i: (0, i)),
            pl.BlockSpec((count, block), lambda i: (0, i)),
        ],
        out_specs=pl.BlockSpec((count, block), lambda i: (0, i)),
        out_shape=jax.ShapeDtypeStruct((count, width), jnp.bfloat16),
        compiler_params=pltpu.CompilerParams(vmem_limit_bytes=56 * 1024 * 1024),
        cost_estimate=pl.CostEstimate(
            flops=2 * count * depth * width,
            bytes_accessed=2 * (depth * width + count * (depth + 2 * width)),
            transcendentals=count * width,
        ),
    )(tokens, weight, cotangent)


def spread(block, axis, groups=None):
    count = lax.axis_size(axis) if groups is None else len(groups[0])
    copies = jnp.broadcast_to(block[None], (count,) + block.shape)
    return lax.all_to_all(copies, axis, 0, 0, tiled=True, axis_index_groups=groups)


def ring_permutes(axis, step):
    count = lax.axis_size(axis)
    ahead = [((i + step) % count, i) for i in range(count)]
    behind = [(i, (i + step) % count) for i in range(count)]
    return (lambda x: lax.ppermute(x, axis, ahead)), (lambda x: lax.ppermute(x, axis, behind))


def by_class(blocks, place):
    count = len(blocks)
    stacked = jnp.stack(blocks)
    return [
        lax.dynamic_index_in_dim(stacked, lax.rem(wanted - place + count, count), 0, keepdims=False)
        for wanted in range(count)
    ]


def local(tokens, cotangent, weight, basis, first_moment, second_moment):
    f32, bf16 = jnp.float32, jnp.bfloat16
    outer, inner, quarters = lax.axis_size("dp"), lax.axis_size("fsdp"), lax.axis_size("tensor")
    rows, width = weight.shape
    rank = basis.shape[1]
    depth = outer * inner * rows
    share = rank // (outer * inner)
    far = outer // RING
    basis_perm = (
        basis.reshape(rows, far, RING, inner, share).transpose(0, 3, 2, 1, 4).reshape(rows, rank)
    )
    part = rank // quarters
    basis_part = lax.dynamic_slice_in_dim(basis_perm, lax.axis_index("tensor") * part, part, 1)

    pairs = [[PAIR * y + x for x in range(PAIR)] for y in range(RING)]
    columns = [[PAIR * y + x for y in range(RING)] for x in range(PAIR)]
    strides = [[i + RING * j for j in range(far)] for i in range(RING)]
    fours = [[RING * j + i for i in range(RING)] for j in range(far)]
    pair_rows = PAIR * rows
    half = width * 9 // 14
    first = jnp.concatenate([weight[:, :half], basis_part], axis=1)
    plane = spread(first, "fsdp").reshape(inner * rows, half + part)
    spare = -(half + part) % LANES
    moments = jnp.concatenate([first_moment, second_moment]).astype(bf16).reshape(-1, spare)
    moments = jnp.pad(moments, ((0, inner * rows - moments.shape[0]), (0, 0)))
    plane = jnp.concatenate([plane, moments], axis=1)
    full_a = lax.all_gather(plane, "dp", axis=0, tiled=True)
    plane, second = lax.optimization_barrier((plane, weight[:, half:]))
    second = spread(second, "fsdp", pairs).reshape(pair_rows, width - half)
    line = lax.all_gather(second, "dp", axis=0)
    from_ahead, from_behind = ring_permutes("fsdp", PAIR)
    ahead, behind = from_ahead(line), from_behind(line)
    across = from_ahead(ahead[: outer // 2]), from_behind(behind[outer // 2 :])

    def grad_of_preact(side, wanted):
        preact = jnp.dot(tokens, side, preferred_element_type=f32)
        return (wanted.astype(f32) * silu_slope(preact)).astype(bf16)

    weight_a, full_basis = full_a[:, :half], full_a[:, half : half + part]
    projected_part = lax.dot_general(
        full_basis, tokens, (((0,), (1,)), ((), ())), preferred_element_type=f32
    ).astype(bf16)
    projected = spread(projected_part, "tensor").reshape(rank, tokens.shape[0])
    grad_pre_a = grad_of_first(tokens, full_a, cotangent, half)
    blocks = by_class([line, ahead, jnp.concatenate(across), behind], lax.axis_index("fsdp") // PAIR)
    weight_b = jnp.stack(blocks, axis=1).reshape(depth, width - half)
    grad_pre_b = grad_of_preact(weight_b, cotangent[:, half:])
    grad_part = jnp.concatenate(
        [
            jnp.dot(projected, g, preferred_element_type=f32).astype(bf16)
            for g in (grad_pre_a, grad_pre_b)
        ],
        axis=1,
    )
    partial_rows = sum(
        lax.dot_general(g, w, (((1,), (1,)), ((), ())), preferred_element_type=f32)
        for g, w in ((grad_pre_a, weight_a), (grad_pre_b, weight_b))
    ).astype(bf16)

    landed = lax.all_to_all(grad_part.reshape(inner, outer * share, width), "fsdp", 0, 0, tiled=True)
    landed, partial_rows = lax.optimization_barrier((landed, partial_rows))
    token_rows = lax.psum_scatter(partial_rows, "tensor", scatter_dimension=0, tiled=True)
    inner_sum = jnp.sum(landed.astype(f32), axis=0)
    blocks = inner_sum.astype(bf16).reshape(RING, far * share, width)
    landed = lax.all_to_all(blocks, "dp", 0, 0, tiled=True, axis_index_groups=fours)
    blocks = jnp.sum(landed.astype(f32), axis=0).astype(bf16)
    landed = spread(blocks, "dp", strides)
    old = full_a[:, half + part :].reshape(far, RING, inner * rows, spare)
    old = lax.dynamic_index_in_dim(old, lax.rem(lax.axis_index("dp"), RING), 1, keepdims=False)
    old = old[:, : 2 * share * width // spare].reshape(far, 2, share, width).astype(f32)
    old_first, old_second = old[:, 0], old[:, 1]
    old_first, token_rows = lax.optimization_barrier((BETA_ONE * old_first, token_rows))
    token_grad = lax.all_gather(token_rows, "tensor", axis=0, tiled=True)
    reduced = jnp.sum(landed.astype(f32), axis=0).reshape(far, share, width)

    token_count = tokens.shape[0] * outer * inner
    grad_low = reduced / float(token_count)
    new_first = old_first + (1.0 - BETA_ONE) * grad_low
    new_second = BETA_TWO * old_second + (1.0 - BETA_TWO) * grad_low * grad_low
    first_hat = new_first / (1.0 - BETA_ONE**ADAM_STEP)
    second_hat = new_second / (1.0 - BETA_TWO**ADAM_STEP)
    direction = (first_hat / (jnp.sqrt(second_hat) + EPSILON)).astype(bf16)
    own = lax.dynamic_index_in_dim(grad_low, lax.axis_index("dp") // RING, 0, keepdims=False)
    new_first_moment = BETA_ONE * first_moment + (1.0 - BETA_ONE) * own
    new_second_moment = BETA_TWO * second_moment + (1.0 - BETA_TWO) * own * own
    column = spread(direction.reshape(far * share, width), "fsdp", pairs)
    column = spread(column.reshape(PAIR * far * share, width), "dp", fours)
    column = column.reshape(PAIR * outer * share, width)
    full_direction = spread(column, "fsdp", columns).reshape(rank, width)
    token_grad = token_grad * lax.optimization_barrier(jnp.ones((), bf16))
    full_direction, token_grad = lax.optimization_barrier((full_direction, token_grad))
    basis_last = (
        basis.reshape(rows, far, RING, RING, PAIR, share)
        .transpose(0, 3, 2, 4, 1, 5)
        .reshape(rows, rank)
    )
    update = jnp.dot(basis_last, full_direction, preferred_element_type=f32)
    new_weight = (weight.astype(f32) - LEARN_RATE * update).astype(bf16)
    return (token_grad, new_weight, new_first_moment, new_second_moment)


def solution(mesh):
    in_specs = (
        P(("dp", "fsdp"), None),
        P(("dp", "fsdp"), "tensor"),
        P(("dp", "fsdp"), "tensor"),
        P(("dp", "fsdp"), None),
        P(("dp", "fsdp"), "tensor"),
        P(("dp", "fsdp"), "tensor"),
    )
    out_specs = (
        P(("dp", "fsdp"), None),
        P(("dp", "fsdp"), "tensor"),
        P(("dp", "fsdp"), "tensor"),
        P(("dp", "fsdp"), "tensor"),
    )
    return jax.shard_map(local, mesh=mesh, in_specs=in_specs, out_specs=out_specs, check_vma=False)
```
